512 devices in a mesh: dp: 8 (over y), expert: 64 (over x, z, core).
Axes of the slice: x: 4, y: 8, z: 8, core: 2. Of those that a mesh axis runs over, the one named last changes fastest.
Arguments:
- tokens: bfloat16 [32768, 1024], P(('dp', 'expert')), may hold values from -6 to 6
- expert_ids: int32 [32768, 8], P(('dp', 'expert')), may hold values from 0 to 63, all different within a row; in each aligned block of 64 rows (0 to 63, 64 to 127, ...) at most 10 rows name the same one
- gate_values: float32 [32768, 8], P(('dp', 'expert')), may hold values from 0.05 to 0.5
- cotangent: bfloat16 [32768, 1024], P(('dp', 'expert')), may hold values from -6 to 6
- w_gate: bfloat16 [64, 1024, 512], P('expert'), may hold values from -0.1875 to 0.1875
- w_up: bfloat16 [64, 1024, 512], P('expert'), may hold values from -0.1875 to 0.1875
- w_down: bfloat16 [64, 512, 1024], P('expert'), may hold values from -0.25 to 0.25
Outputs:
- layer_output: bfloat16 [32768, 1024], P(('dp', 'expert'))
- d_tokens: bfloat16 [32768, 1024], P(('dp', 'expert'))
- d_gate_w: float32 [64, 1024, 512], P('expert', 'dp')
- d_up_w: float32 [64, 1024, 512], P('expert', 'dp')
- d_down_w: float32 [64, 512, 1024], P('expert', None, 'dp')
The draws below stay inside these ranges and needn't reach their ends.
Inputs may be any that keep to these rules, and one draw needn't show every extreme that they name: `expert_ids`: the 8 ids of a row are distinct. In each aligned block of 64 rows (the tokens of one device) no expert is named by more than 10 rows, a bound that some block reaches.
All inputs are finite; a program needn't handle non-finite values.
Results may differ from the reference program's by a relative error of at most 0.015.
Values may be sent and summed in bfloat16 or wider, within the bound.
A program may use at most 64 MiB of HBM per device.

```python
import math
import jax
import jax.numpy as jnp
import numpy as np
from jax import lax

D = 1024
FF = 512
TOP = 8
TOK_DEV = 64
EXPERTS = 64
CAP = 10
TOKENS = 32768
N_DP = 8
N_EXPERT = 64


def level_of(own_key, dims, shards, least, high):
    level, own = 1.0, jax.random.fold_in(own_key, 6)
    for position, parts in shards:
        steps = jnp.exp(jax.random.uniform(jax.random.fold_in(own, position), (parts,), jnp.float32, least / len(shards), high / len(shards)))
        level = level * jnp.repeat(steps, dims[position] // parts).reshape([-1 if axis == position else 1 for axis in range(len(dims))])
    return level


def shared_out(rng, own, number, rows, number_of, top, most, skew):
    order = jax.random.permutation(rng, number_of)
    packed, common = shares(number_of, rows * top, most, skew, True), shares(number_of, rows * top, most, skew, False)
    places = jnp.arange(number_of)

    def named(lengths, rotation):
        used = int((lengths > 0).sum())
        fixed = max(1, used // 4)
        shifted = fixed + (places - fixed + rotation * (used - fixed)) % max(1, number_of - fixed)
        return jnp.zeros((number_of,), jnp.int32).at[order[jnp.where(places < fixed, places, shifted)]].set(jnp.asarray(lengths, jnp.int32))

    lengths = jnp.where(number % 4 == 0, named(packed, number // 4), named(common, number - number // 4 - 1))
    mixed = jax.random.permutation(jax.random.fold_in(own, 3), number_of)
    giver, taker = mixed[0:number_of // 2 * 2:2], mixed[1:number_of // 2 * 2:2]
    room = jnp.minimum(lengths[giver] - 1, most - lengths[taker]) // 2
    room = jnp.where((giver == order[0]) | (taker == order[0]) | (lengths[taker] == 0), 0, jnp.maximum(room, 0))
    shifted = jax.random.randint(jax.random.fold_in(own, 4), (number_of // 2,), 0, 1 << 20) % (room + 1)
    lengths = lengths.at[giver].add(-shifted).at[taker].add(shifted)
    labels = jnp.searchsorted(jnp.cumsum(lengths), jnp.arange(rows * top), side="right").astype(jnp.int32)
    grid = labels.reshape(top, rows).T
    grid = grid[jax.random.permutation(jax.random.fold_in(own, 1), rows)]
    rotation = jax.random.randint(jax.random.fold_in(own, 2), (rows, 1), 0, top)
    return jnp.take_along_axis(grid, (jnp.arange(top)[None, :] + rotation) % top, axis=1)


def shares(amount, total, limit, skew, full):
    loads = [(1 << 20) // math.isqrt(standing ** skew) + 1 for standing in range(1, amount + 1)]
    largest = limit if full else min(limit, max(-(-total // amount), total * loads[0] // sum(loads)))
    least = 1 if total - largest >= amount - 1 else 0
    holding, rest = [largest] + [least] * (amount - 1), total - largest - least * (amount - 1)
    while rest > 0:
        candidates = [i for i in range(1, amount) if holding[i] < largest] or [i for i in range(1, amount) if holding[i] < limit]
        pool, remaining = sum([loads[i] for i in candidates]), rest
        for i in candidates:
            extra = min(limit - holding[i], max(1, remaining * loads[i] // pool), rest)
            holding[i] = holding[i] + extra
            rest = rest - extra
    return np.array(holding)


def bell_draw(own_key, shape, spread, most, cuts=(), held_as=jnp.bfloat16):
    result = jax.random.normal(own_key, shape, jnp.float32) * spread
    if len(cuts) > 0:
        result = level_of(own_key, shape, cuts, -0.22, 0.18) * result
    return jnp.clip(result, min=-most, max=most).astype(held_as)


def setup_inputs(seed: int = 0) -> dict:
    arg_keys = jax.random.split(jax.random.key(seed), 8)
    tokens = bell_draw(arg_keys[0], (TOKENS, D), 1.0, 6.0, ((0, 512),))
    expert_ids_keys = jax.random.split(jax.random.fold_in(arg_keys[1], 1), TOKENS // TOK_DEV)
    expert_ids_turns = jax.random.permutation(jax.random.fold_in(arg_keys[1], 3), TOKENS // TOK_DEV)
    expert_ids = jax.vmap(lambda own, number: shared_out(jax.random.fold_in(arg_keys[1], 2), own, number, TOK_DEV, EXPERTS, TOP, CAP, 2))(expert_ids_keys, expert_ids_turns).reshape((TOKENS, TOP))
    gate_values = jnp.clip(0.05 + 0.45 * jax.random.uniform(arg_keys[2], (TOKENS, TOP), jnp.float32) ** level_of(arg_keys[2], (TOKENS, TOP), ((0, 512),), -0.2, 0.2), 0.05, 0.5)
    cotangent = bell_draw(arg_keys[3], (TOKENS, D), 1.0, 6.0, ((0, 512),))
    w_gate = bell_draw(arg_keys[4], (EXPERTS, D, FF), D ** -0.5, 0.1875, ((0, 64),))
    w_up = bell_draw(arg_keys[5], (EXPERTS, D, FF), D ** -0.5, 0.1875, ((0, 64),))
    w_down = bell_draw(arg_keys[6], (EXPERTS, FF, D), FF ** -0.5, 0.25, ((0, 64),))
    return {"tokens": tokens, "expert_ids": expert_ids, "gate_values": gate_values, "cotangent": cotangent, "w_gate": w_gate, "w_up": w_up, "w_down": w_down}


def reference(tokens, expert_ids, gate_values, cotangent, w_gate, w_up, w_down):
    group_tokens = TOK_DEV * N_EXPERT
    window = N_EXPERT * CAP
    token_groups = tokens.reshape(N_DP, group_tokens, D)
    id_groups = expert_ids.reshape(N_DP, group_tokens, TOP)
    gate_groups = gate_values.reshape(N_DP, group_tokens, TOP)
    grad_groups = cotangent.reshape(N_DP, group_tokens, D)

    def group_pass(totals, inputs):
        features, routes, weights, out_grad = inputs
        flat_ids = routes.reshape(-1).astype(jnp.int32)
        sorted_pairs = jnp.argsort(flat_ids, stable=True).astype(jnp.int32)
        counts = jnp.sum((flat_ids[:, None] == jnp.arange(EXPERTS, dtype=jnp.int32)[None, :]).astype(jnp.int32), axis=0)
        starts = (jnp.cumsum(counts) - counts).astype(jnp.int32)
        padded_pairs = jnp.concatenate([sorted_pairs, jnp.zeros((window,), jnp.int32)])
        scaled_all = (weights[:, :, None] * out_grad[:, None, :].astype(jnp.float32)).astype(jnp.bfloat16)

        def expert_step(sums, expert_index):
            output_sum, input_sum = sums
            pair_index = lax.dynamic_slice_in_dim(padded_pairs, starts[expert_index], window)
            valid_rows = jnp.arange(window, dtype=jnp.int32) < counts[expert_index]
            token_index = (pair_index // TOP).astype(jnp.int32)
            rank_index = (pair_index % TOP).astype(jnp.int32)
            input_rows = jnp.where(valid_rows[:, None], features[token_index], jnp.zeros((), features.dtype))
            grad_rows = jnp.where(valid_rows[:, None], scaled_all[token_index, rank_index], jnp.zeros((), scaled_all.dtype))
            gate_share = jnp.where(valid_rows, weights[token_index, rank_index], jnp.zeros((), weights.dtype))
            gate_mat = w_gate[expert_index]
            up_mat = w_up[expert_index]
            down_mat = w_down[expert_index]
            gate_pre = jnp.dot(input_rows, gate_mat, preferred_element_type=jnp.float32)
            up_pre = jnp.dot(input_rows, up_mat, preferred_element_type=jnp.float32)
            sigmoid_gate = jax.nn.sigmoid(gate_pre)
            activation = (gate_pre * sigmoid_gate * up_pre).astype(jnp.bfloat16)
            produced = jnp.dot(activation, down_mat, preferred_element_type=jnp.float32).astype(jnp.bfloat16)
            output_sum = output_sum.at[token_index].add(gate_share[:, None].astype(jnp.float32) * produced.astype(jnp.float32))
            d_activation = jnp.dot(grad_rows, down_mat.T, preferred_element_type=jnp.float32)
            d_up_pre = (d_activation * gate_pre * sigmoid_gate).astype(jnp.bfloat16)
            d_gate_pre = (d_activation * up_pre * sigmoid_gate * (1.0 + gate_pre * (1.0 - sigmoid_gate))).astype(jnp.bfloat16)
            input_grads = (jnp.dot(d_gate_pre, gate_mat.T, preferred_element_type=jnp.float32)
                           + jnp.dot(d_up_pre, up_mat.T, preferred_element_type=jnp.float32)).astype(jnp.bfloat16)
            input_sum = input_sum.at[token_index].add(jnp.where(valid_rows[:, None], input_grads.astype(jnp.float32), jnp.zeros((), jnp.float32)))
            gate_grad = jnp.dot(input_rows.T, d_gate_pre, preferred_element_type=jnp.float32).astype(jnp.bfloat16)
            up_grad = jnp.dot(input_rows.T, d_up_pre, preferred_element_type=jnp.float32).astype(jnp.bfloat16)
            down_grad = jnp.dot(activation.T, grad_rows, preferred_element_type=jnp.float32).astype(jnp.bfloat16)
            return (output_sum, input_sum), (gate_grad, up_grad, down_grad)

        start_sums = (jnp.zeros((group_tokens, D), jnp.float32), jnp.zeros((group_tokens, D), jnp.float32))
        (output_sum, input_sum), (gate_parts, up_parts, down_parts) = lax.scan(expert_step, start_sums, jnp.arange(EXPERTS, dtype=jnp.int32))
        totals = (totals[0] + gate_parts.astype(jnp.float32), totals[1] + up_parts.astype(jnp.float32), totals[2] + down_parts.astype(jnp.float32))
        return totals, (output_sum.astype(jnp.bfloat16), input_sum.astype(jnp.bfloat16))

    start_totals = (jnp.zeros((EXPERTS, D, FF), jnp.float32), jnp.zeros((EXPERTS, D, FF), jnp.float32), jnp.zeros((EXPERTS, FF, D), jnp.float32))
    (d_gate_w, d_up_w, d_down_w), (layer_output, d_tokens) = lax.scan(group_pass, start_totals, (token_groups, id_groups, gate_groups, grad_groups))
    return layer_output.reshape(TOKENS, D), d_tokens.reshape(TOKENS, D), d_gate_w, d_up_w, d_down_w
```

```python
import jax
import jax.numpy as jnp
from jax import lax
from jax.experimental import pallas as pl
from jax.experimental.pallas import tpu as pltpu
from jax.sharding import PartitionSpec as P

MESH = pl.DeviceIdType.MESH
BF = jnp.bfloat16
F32 = jnp.float32
NX, NZ, NC = 4, 8, 2
NY = 8
TOK = 64
D = 1024
HALF = D // 2
FF = 512
CAP = 10
SLOTS = NZ * CAP
PEERS = NX * NC
ROWS = PEERS * SLOTS
GATHERED = NZ * TOK
EXPERTS = NX * NZ * NC
TILE = 160
STEPS = ((4, 3), (3, 4))
WROWS = 192


def nn(a, b):
    return jnp.dot(a, b, preferred_element_type=F32)


def nt(a, b):
    return lax.dot_general(a, b, (((1,), (1,)), ((), ())), preferred_element_type=F32)


def tn(a, b):
    return lax.dot_general(a, b, (((0,), (0,)), ((), ())), preferred_element_type=F32)


def kernel(
    ids_ref, gv_ref, tok_ref, cot_ref, wg_ref, wu_ref, wd_ref,
    out_ref, dtok_ref, dg_ref, du_ref, dd_ref,
    meta, gath, pick, pick_t, pickg_t, gslot, send_x, recv_x, keep_s, keep_d, act, dpre, part, zbuf, wpart, ybuf,
    m_ss, m_rs, g_ss, g_rs, x_ss, x_rs, z_ss, z_rs, y_ss, y_rs,
):
    y = lax.axis_index("dp")
    e = lax.axis_index("expert")
    c = e % 2
    z = (e // 2) % NZ
    x = e // (2 * NZ)
    up = (y, (x * NZ + (z + 1) % NZ) * 2 + c)
    down = (y, (x * NZ + (z + NZ - 1) % NZ) * 2 + c)
    y_up = ((y + 1) % NY, e)
    y_down = ((y + NY - 1) % NY, e)

    def peer(j, sign):
        dx, dc = j // 2, j % 2
        return (y, (((x + sign * dx + NX) % NX) * NZ + z) * 2 + (c + dc) % 2)

    barrier = pltpu.get_barrier_semaphore()
    friends = [up, down, y_up, y_down] + [peer(j, 1) for j in range(1, PEERS)]
    for friend in friends:
        pl.semaphore_signal(barrier, inc=1, device_id=friend, device_id_type=MESH)

    lane = lax.broadcasted_iota(jnp.int32, (TOK, 2 * EXPERTS), 1)
    gate = jnp.zeros((TOK, 2 * EXPERTS), F32)
    for k in range(8):
        gate = jnp.where(lane % EXPERTS == ids_ref[:, k : k + 1], gv_ref[:, k : k + 1], gate)
    high = gate.astype(BF).astype(F32)
    meta[0] = jnp.where(lane < EXPERTS, high, gate - high).astype(BF)
    for h in range(2):
        gath[0, h, 0] = tok_ref[:, h * HALF : (h + 1) * HALF]
        gath[1, h, 0] = cot_ref[:, h * HALF : (h + 1) * HALF]

    pl.semaphore_wait(barrier, len(friends))

    started = []

    def send(src, dst, ss, rs, to):
        copy = pltpu.make_async_remote_copy(
            src_ref=src, dst_ref=dst, send_sem=ss, recv_sem=rs, device_id=to, device_id_type=MESH
        )
        copy.start()
        started.append(copy)
        return copy

    def gather_step(buf, ss, rs, steps, s, prev):
        now = []
        for way, (to, count) in enumerate(zip((up, down), steps)):
            if s > count:
                now.append(None)
                continue
            if s > 1:
                prev[way].wait_recv()
            src = (NZ - s + 1) % NZ if way == 0 else s - 1
            dst = NZ - s if way == 0 else s
            now.append(send(buf.at[src], buf.at[dst], ss.at[dst], rs.at[dst], to))
        return [n if n is not None else p for n, p in zip(now, prev or (None, None))]

    m_last, t_last, c_last = None, [None, None], [None, None]
    for s in range(1, 5):
        m_last = gather_step(meta, m_ss, m_rs, STEPS[0], s, m_last)
        for h in range(2):
            t_last[h] = gather_step(gath.at[0, h], g_ss.at[0, h], g_rs.at[0, h], STEPS[h], s, t_last[h])
    for h in range(2):
        c_last[h] = gather_step(gath.at[1, h], g_ss.at[1, h], g_rs.at[1, h], STEPS[h], 1, None)

    for way in range(2):
        m_last[way].wait_recv()
    row = lax.broadcasted_iota(jnp.int32, (16, 2 * EXPERTS), 0)
    col = lax.broadcasted_iota(jnp.int32, (16, 2 * EXPERTS), 1)
    wanted = (((x + (row % PEERS) // 2) % NX) * NZ + z) * 2 + (c + row) % 2
    chosen = jnp.where(col % EXPERTS == wanted, 1.0, 0.0).astype(BF)
    gate_row = nt(chosen, meta[...].reshape(GATHERED, 2 * EXPERTS))
    match = jnp.where(gate_row > 0.0, 1.0, 0.0)
    first = lax.broadcasted_iota(jnp.int32, (GATHERED, GATHERED), 0)
    second = lax.broadcasted_iota(jnp.int32, (GATHERED, GATHERED), 1)
    rank = nn(match.astype(BF), jnp.where(first < second, 1.0, 0.0).astype(BF))
    place = jnp.where(gate_row > 0.0, rank, -1.0)
    slot = lax.broadcasted_iota(jnp.int32, (SLOTS, GATHERED), 0).astype(F32)
    for j in range(PEERS):
        hit = slot == place[j : j + 1, :]
        pick[j * SLOTS : (j + 1) * SLOTS, :] = jnp.where(hit, 1.0, 0.0).astype(BF)
        weight = jnp.sum(jnp.where(hit, gate_row[j : j + 1, :], 0.0), axis=1, keepdims=True)
        gslot[j * SLOTS : (j + 1) * SLOTS, :] = jnp.broadcast_to(weight, (SLOTS, 128))

    for h in range(2):
        for way in range(2):
            t_last[h][way].wait_recv()

    def tiles(body):
        def step(i, carry):
            body(pl.ds(pl.multiple_of(i * TILE, 16), TILE))
            return carry

        lax.fori_loop(0, ROWS // TILE, step, 0)

    def exchange(n, src, dst, sign):
        own = pl.ds(0, SLOTS)
        dst[own, :] = src[own, :]
        copies = []
        for j in (4, 5, 2, 3, 6, 7, 1):
            block = pl.ds(j * SLOTS, SLOTS)
            copies.append(send(src.at[block], dst.at[block], x_ss.at[n, j], x_rs.at[n, j], peer(j, sign)))
        return copies

    def pick_tokens(rows):
        for h in range(2):
            source = gath[0, h].reshape(GATHERED, HALF)
            send_x[0, rows, h * HALF : (h + 1) * HALF] = nn(pick[rows, :], source).astype(BF)

    tiles(pick_tokens)
    tok_moves = exchange(0, send_x.at[0], recv_x.at[0], 1)

    for s in range(2, 5):
        for h in range(2):
            c_last[h] = gather_step(gath.at[1, h], g_ss.at[1, h], g_rs.at[1, h], STEPS[h], s, c_last[h])
    for h in range(2):
        for way in range(2):
            c_last[h][way].wait_recv()

    def pick_grads(rows):
        for h in range(2):
            source = gath[1, h].reshape(GATHERED, HALF)
            scaled = nn(pick[rows, :], source) * gslot[rows, 0:1]
            send_x[1, rows, h * HALF : (h + 1) * HALF] = scaled.astype(BF)

    tiles(pick_grads)
    cot_moves = exchange(1, send_x.at[1], recv_x.at[1], 1)

    for q in range(4):
        cols = slice(q * 128, (q + 1) * 128)
        plain = pick[:, cols].astype(F32)
        pick_t[cols, :] = plain.T.astype(BF)
        pickg_t[cols, :] = (plain * gslot[...]).T.astype(BF)

    for move in tok_moves:
        move.wait_recv()

    def forward(rows):
        inp = recv_x[0, rows, :]
        g = nn(inp, wg_ref[...])
        u = nn(inp, wu_ref[...])
        s = jax.nn.sigmoid(g)
        silu = g * s
        keep_s[rows, :] = silu
        keep_d[rows, :] = u * s * (1.0 + g * (1.0 - s))
        a = (silu * u).astype(BF)
        act[rows, :] = a
        send_x[2, rows, :] = nn(a, wd_ref[...]).astype(BF)

    tiles(forward)

    for move in cot_moves:
        move.wait_recv()
    out_moves = exchange(2, send_x.at[2], recv_x.at[2], -1)

    def backward(rows):
        da = nt(recv_x[1, rows, :], wd_ref[...])
        d_up = (da * keep_s[rows, :]).astype(BF)
        d_gate = (da * keep_d[rows, :]).astype(BF)
        dpre[rows, 0:FF] = d_gate
        dpre[rows, FF : 2 * FF] = d_up
        send_x[3, rows, :] = (nt(d_gate, wg_ref[...]) + nt(d_up, wu_ref[...])).astype(BF)

    tiles(backward)
    grad_moves = exchange(3, send_x.at[3], recv_x.at[3], -1)

    def weight_part(k):
        cols = pl.ds(pl.multiple_of(((y + k) % NY) * 128, 128), 128)
        both = tn(recv_x[0, :, cols], dpre[...])
        wpart[k, 0:128, :] = both[:, 0:FF]
        wpart[k, 128:256, :] = both[:, FF : 2 * FF]
        wpart[k, 256:384, :] = tn(recv_x[1, :, cols], act[...])

    def reduce_step(buf, ss, rs, ways, h, s, prev, own):
        now = []
        for way in range(2):
            count = STEPS[h][way]
            if s > count:
                now.append(prev[way])
                continue
            ahead = count + 1 - s
            term = own(ahead if way == 0 else 8 - ahead, h)
            if s > 1:
                prev[way].wait_recv()
                term = term + buf[h, way, s - 1].astype(F32)
            buf[h, way, s - 1] = term.astype(BF)
            now.append(
                send(buf.at[h, way, s - 1], buf.at[h, way, s], ss.at[h, way, s], rs.at[h, way, s], ways[way])
            )
        return now

    def reduce_end(buf, h, prev, own):
        for way in range(2):
            prev[way].wait_recv()
        first, second = STEPS[h]
        return own(0, h) + buf[h, 0, first].astype(F32) + buf[h, 1, second].astype(F32)

    def own_w(k, h):
        return wpart[k, h * WROWS : (h + 1) * WROWS, :]

    def own_part(a):
        return lambda k, h: part[a, k * TOK : (k + 1) * TOK, h * HALF : (h + 1) * HALF]

    y_last, z_last = [None, None], [[None, None], [None, None]]

    def y_step(s):
        for h in range(2):
            y_last[h] = reduce_step(ybuf, y_ss, y_rs, (y_up, y_down), h, s, y_last[h], own_w)

    def z_step(a, s):
        for h in range(2):
            z_last[a][h] = reduce_step(
                zbuf.at[a], z_ss.at[a], z_rs.at[a], (up, down), h, s, z_last[a][h], own_part(a)
            )

    def combine(a, weights, moves):
        for move in moves:
            move.wait_recv()

        def step(i, carry):
            rows = pl.ds(pl.multiple_of(i * 128, 128), 128)
            part[a, rows, :] = nn(weights[rows, :], recv_x[2 + a])
            return carry

        lax.fori_loop(0, GATHERED // 128, step, 0)

    def z_end(a, result):
        for h in range(2):
            result[:, h * HALF : (h + 1) * HALF] = reduce_end(zbuf.at[a], h, z_last[a][h], own_part(a)).astype(BF)

    weight_part(4)
    weight_part(3)
    weight_part(5)
    y_step(1)
    combine(0, pickg_t, out_moves)
    z_step(0, 1)
    for k in (2, 6, 1, 7, 0):
        weight_part(k)
    z_step(0, 2)
    y_step(2)
    z_step(0, 3)
    z_step(0, 4)
    combine(1, pick_t, grad_moves)
    z_step(1, 1)
    y_step(3)
    z_step(1, 2)
    z_end(0, out_ref)
    z_step(1, 3)
    y_step(4)
    z_step(1, 4)
    z_end(1, dtok_ref)
    low = reduce_end(ybuf, 0, y_last[0], own_w)
    dg_ref[...] = low[0:128]
    du_ref[0:64] = low[128:192]
    rest = reduce_end(ybuf, 1, y_last[1], own_w)
    du_ref[64:128] = rest[0:64]
    dd_ref[...] = rest[64:192].T

    for copy in started:
        copy.wait_send()


def on_device(tokens, expert_ids, gate_values, cotangent, w_gate, w_up, w_down):
    vmem = pl.BlockSpec(memory_space=pltpu.VMEM)
    dma = pltpu.SemaphoreType.DMA
    out, dtok, dg, du, dd = pl.pallas_call(
        kernel,
        out_shape=(
            jax.ShapeDtypeStruct((TOK, D), BF),
            jax.ShapeDtypeStruct((TOK, D), BF),
            jax.ShapeDtypeStruct((128, FF), F32),
            jax.ShapeDtypeStruct((128, FF), F32),
            jax.ShapeDtypeStruct((FF, 128), F32),
        ),
        in_specs=[vmem] * 7,
        out_specs=(vmem,) * 5,
        scratch_shapes=[
            pltpu.VMEM((NZ, TOK, 2 * EXPERTS), BF),
            pltpu.VMEM((2, 2, NZ, TOK, HALF), BF),
            pltpu.VMEM((ROWS, GATHERED), BF),
            pltpu.VMEM((GATHERED, ROWS), BF),
            pltpu.VMEM((GATHERED, ROWS), BF),
            pltpu.VMEM((ROWS, 128), F32),
            pltpu.VMEM((4, ROWS, D), BF),
            pltpu.VMEM((4, ROWS, D), BF),
            pltpu.VMEM((ROWS, FF), F32),
            pltpu.VMEM((ROWS, FF), F32),
            pltpu.VMEM((ROWS, FF), BF),
            pltpu.VMEM((ROWS, 2 * FF), BF),
            pltpu.VMEM((2, GATHERED, D), F32),
            pltpu.VMEM((2, 2, 2, 5, TOK, HALF), BF),
            pltpu.VMEM((NY, 2 * WROWS, FF), F32),
            pltpu.VMEM((2, 2, 5, WROWS, FF), BF),
            dma((NZ,)), dma((NZ,)),
            dma((2, 2, NZ)), dma((2, 2, NZ)),
            dma((4, PEERS)), dma((4, PEERS)),
            dma((2, 2, 2, 5)), dma((2, 2, 2, 5)),
            dma((2, 2, 5)), dma((2, 2, 5)),
        ],
        compiler_params=pltpu.CompilerParams(
            collective_id=0, has_side_effects=True, vmem_limit_bytes=58 * 1024 * 1024
        ),
        cost_estimate=pl.CostEstimate(flops=7_000_000_000, bytes_accessed=8_000_000, transcendentals=400_000),
    )(expert_ids, gate_values, tokens, cotangent, w_gate[0], w_up[0], w_down[0])
    return out, dtok, dg[None], du[None], dd[None]


def solution(mesh):
    rows = P(("dp", "expert"), None)
    weights = P("expert", None, None)
    return jax.shard_map(
        on_device,
        mesh=mesh,
        in_specs=(rows,) * 4 + (weights,) * 3,
        out_specs=(rows, rows, P("expert", "dp", None), P("expert", "dp", None), P("expert", None, "dp")),
        check_vma=False,
    )
```

```python
import jax
import jax.numpy as jnp
from jax import lax
from jax.experimental import pallas as pl
from jax.experimental.pallas import tpu as pltpu
from jax.sharding import PartitionSpec as P

MESH = pl.DeviceIdType.MESH
BF = jnp.bfloat16
F32 = jnp.float32
NX, NZ, NC = 4, 8, 2
NY = 8
TOK = 64
D = 1024
HALF = D // 2
FF = 512
CAP = 10
SLOTS = NZ * CAP
PEERS = NX * NC
ROWS = PEERS * SLOTS
GATHERED = NZ * TOK
EXPERTS = NX * NZ * NC
WIDE = 256
STEPS = ((4, 3), (3, 4))
WSTEPS = ((3, 4), (4, 3), (4, 3))


def nn(a, b):
    return jnp.dot(a, b, preferred_element_type=F32)


def nt(a, b):
    return lax.dot_general(a, b, (((1,), (1,)), ((), ())), preferred_element_type=F32)


def tn(a, b):
    return lax.dot_general(a, b, (((0,), (0,)), ((), ())), preferred_element_type=F32)


def kernel(
    ids_ref, gv_ref, tok_ref, cot_ref, wg_hbm, wu_hbm, wd_hbm,
    out_ref, dtok_ref, dg_ref, du_ref, dd_ref,
    meta, gath, pick, pick_t, pickg_t, gslot, send_x, recv_x, keep_s, keep_d, act, dpre, part, zbuf, wboth, wdown, yboth, ydown, act_t, tok_t, wg_ref, wu_ref, wd_ref,
    m_ss, m_rs, g_ss, g_rs, x_ss, x_rs, z_ss, z_rs, y_ss, y_rs, w_s,
):
    y = lax.axis_index("dp")
    e = lax.axis_index("expert")
    c = e % 2
    z = (e // 2) % NZ
    x = e // (2 * NZ)
    up = (y, (x * NZ + (z + 1) % NZ) * 2 + c)
    down = (y, (x * NZ + (z + NZ - 1) % NZ) * 2 + c)
    y_up = ((y + 1) % NY, e)
    y_down = ((y + NY - 1) % NY, e)

    def peer(j, sign):
        dx, dc = j // 2, j % 2
        return (y, (((x + sign * dx + NX) % NX) * NZ + z) * 2 + (c + dc) % 2)

    loads = [
        pltpu.make_async_copy(src, dst, w_s.at[n])
        for n, (src, dst) in enumerate(((wg_hbm, wg_ref), (wu_hbm, wu_ref), (wd_hbm, wd_ref)))
    ]
    for load in loads:
        load.start()
    barrier = pltpu.get_barrier_semaphore()
    friends = [up, down, y_up, y_down] + [peer(j, 1) for j in range(1, PEERS)]
    for friend in friends:
        pl.semaphore_signal(barrier, inc=1, device_id=friend, device_id_type=MESH)

    line = lax.broadcasted_iota(jnp.int32, (2 * EXPERTS, TOK), 0)
    gate = jnp.zeros((2 * EXPERTS, TOK), F32)
    for k in range(8):
        gate = jnp.where(line % EXPERTS == ids_ref[k : k + 1, :], gv_ref[k : k + 1, :], gate)
    gate = gate.T
    lane = lax.broadcasted_iota(jnp.int32, (TOK, 2 * EXPERTS), 1)
    high = gate.astype(BF).astype(F32)
    meta[0] = jnp.where(lane < EXPERTS, high, gate - high).astype(BF)
    for h in range(2):
        gath[0, h, 0] = tok_ref[:, h * HALF : (h + 1) * HALF]
        gath[1, h, 0] = cot_ref[:, h * HALF : (h + 1) * HALF]

    pl.semaphore_wait(barrier, len(friends))

    started = []

    def send(src, dst, ss, rs, to):
        copy = pltpu.make_async_remote_copy(
            src_ref=src, dst_ref=dst, send_sem=ss, recv_sem=rs, device_id=to, device_id_type=MESH
        )
        copy.start()
        started.append(copy)
        return copy

    def gather_step(buf, ss, rs, steps, s, prev):
        now = []
        for way, (to, count) in enumerate(zip((up, down), steps)):
            if s > count:
                now.append(None)
                continue
            if s > 1:
                prev[way].wait_recv()
            src = (NZ - s + 1) % NZ if way == 0 else s - 1
            dst = NZ - s if way == 0 else s
            now.append(send(buf.at[src], buf.at[dst], ss.at[dst], rs.at[dst], to))
        return [n if n is not None else p for n, p in zip(now, prev or (None, None))]

    m_last, t_last, c_last = None, [None, None], [None, None]
    for s in range(1, 5):
        m_last = gather_step(meta, m_ss, m_rs, STEPS[0], s, m_last)
        for h in range(2):
            t_last[h] = gather_step(gath.at[0, h], g_ss.at[0, h], g_rs.at[0, h], STEPS[h], s, t_last[h])
    for h in range(2):
        c_last[h] = gather_step(gath.at[1, h], g_ss.at[1, h], g_rs.at[1, h], STEPS[h], 1, None)

    for way in range(2):
        m_last[way].wait_recv()
    row = lax.broadcasted_iota(jnp.int32, (16, 2 * EXPERTS), 0)
    col = lax.broadcasted_iota(jnp.int32, (16, 2 * EXPERTS), 1)
    wanted = (((x + (row % PEERS) // 2) % NX) * NZ + z) * 2 + (c + row) % 2
    chosen = jnp.where(col % EXPERTS == wanted, 1.0, 0.0).astype(BF)
    gate_row = nt(chosen, meta[...].reshape(GATHERED, 2 * EXPERTS))
    match = jnp.where(gate_row > 0.0, 1.0, 0.0)
    first = lax.broadcasted_iota(jnp.int32, (GATHERED, GATHERED), 0)
    second = lax.broadcasted_iota(jnp.int32, (GATHERED, GATHERED), 1)
    rank = nn(match.astype(BF), jnp.where(first < second, 1.0, 0.0).astype(BF))
    place = jnp.where(gate_row > 0.0, rank, -1.0)
    slot = lax.broadcasted_iota(jnp.int32, (SLOTS, GATHERED), 0).astype(F32)
    for j in range(PEERS):
        hit = slot == place[j : j + 1, :]
        pick[j * SLOTS : (j + 1) * SLOTS, :] = jnp.where(hit, 1.0, 0.0).astype(BF)
        weight = jnp.sum(jnp.where(hit, gate_row[j : j + 1, :], 0.0), axis=1, keepdims=True)
        gslot[j * SLOTS : (j + 1) * SLOTS, :] = jnp.broadcast_to(weight, (SLOTS, 128))

    for h in range(2):
        for way in range(2):
            t_last[h][way].wait_recv()

    def chunks(count, body):
        def step(i, carry):
            body(pl.ds(pl.multiple_of(i * WIDE, WIDE), WIDE))
            return carry

        lax.fori_loop(0, count, step, 0)

    def exchange(n, sign, begin=0, width=D):
        sem = 4 if begin else n
        cols = pl.ds(begin, width)
        recv_x[n, 0:SLOTS, cols] = send_x[n, 0:SLOTS, cols]
        copies = []
        for j in (4, 5, 2, 3, 6, 7, 1):
            block = pl.ds(j * SLOTS, SLOTS)
            src, dst = send_x.at[n, block, cols], recv_x.at[n, block, cols]
            copies.append(send(src, dst, x_ss.at[sem, j], x_rs.at[sem, j], peer(j, sign)))
        return copies

    def picked(a, h):
        source = gath[a, h].reshape(GATHERED, HALF)
        return nn(pick[...], source)

    for h in range(2):
        send_x[0, :, h * HALF : (h + 1) * HALF] = picked(0, h).astype(BF)
    tok_moves = exchange(0, 1)

    for s in range(2, 5):
        for h in range(2):
            c_last[h] = gather_step(gath.at[1, h], g_ss.at[1, h], g_rs.at[1, h], STEPS[h], s, c_last[h])
    for h in range(2):
        for way in range(2):
            c_last[h][way].wait_recv()

    for h in range(2):
        send_x[1, :, h * HALF : (h + 1) * HALF] = (picked(1, h) * gslot[:, 0:1]).astype(BF)
    cot_moves = exchange(1, 1)

    for q in range(4):
        cols = slice(q * 128, (q + 1) * 128)
        plain = pick[:, cols].astype(F32)
        pick_t[cols, :] = plain.T.astype(BF)
        pickg_t[cols, :] = (plain * gslot[...]).T.astype(BF)

    for load in loads:
        load.wait()
    for move in tok_moves:
        move.wait_recv()

    def forward(cols):
        g = nn(recv_x[0], wg_ref[:, cols])
        u = nn(recv_x[0], wu_ref[:, cols])
        s = jax.nn.sigmoid(g)
        silu = g * s
        keep_s[:, cols] = silu
        keep_d[:, cols] = u * s * (1.0 + g * (1.0 - s))
        act[:, cols] = (silu * u).astype(BF)

    def forward_out(cols):
        send_x[2, :, cols] = nn(act[...], wd_ref[:, cols]).astype(BF)

    chunks(FF // WIDE, forward)
    chunks(D // WIDE, forward_out)
    out_moves = exchange(2, -1)
    for q in range(FF // 128):
        act_t[q * 128 : (q + 1) * 128, :] = act[:, q * 128 : (q + 1) * 128].astype(F32).T.astype(BF)
    for q in range(D // 128):
        tok_t[q * 128 : (q + 1) * 128, :] = recv_x[0, :, q * 128 : (q + 1) * 128].astype(F32).T.astype(BF)
    for move in cot_moves:
        move.wait_recv()

    def weight_down(cols):
        wdown[:, cols] = nn(act_t[...], recv_x[1, :, cols])

    def weight_both(cols):
        wboth[:, cols] = nn(tok_t[...], dpre[:, cols])

    def reduce_step(buf, ss, rs, ways, steps, h, s, prev, own):
        now = []
        for way in range(2):
            count = steps[way]
            if s > count:
                now.append(prev[way])
                continue
            ahead = count + 1 - s
            term = own(ahead if way == 0 else 8 - ahead, h)
            if s > 1:
                prev[way].wait_recv()
                term = term + buf(h, way, s - 1)[...].astype(F32)
            buf(h, way, s - 1)[...] = term.astype(BF)
            now.append(
                send(buf(h, way, s - 1), buf(h, way, s), ss.at[h, way, s], rs.at[h, way, s], ways[way])
            )
        return now

    def reduce_end(buf, steps, h, prev, own):
        for way in range(2):
            prev[way].wait_recv()
        first, second = steps
        return own(0, h) + buf(h, 0, first)[...].astype(F32) + buf(h, 1, second)[...].astype(F32)

    def own_w(k, n):
        there = pl.ds(pl.multiple_of(((y + k) % NY) * 128, 128), 128)
        if n == 2:
            return wdown[:, there]
        return wboth[there, n * FF : (n + 1) * FF]

    def own_part(a):
        return lambda k, h: part[a, k * TOK : (k + 1) * TOK, h * HALF : (h + 1) * HALF]

    def y_buf(n, way, s):
        return ydown.at[way, s] if n == 2 else yboth.at[n, way, s]

    def z_buf(a):
        return lambda h, way, s: zbuf.at[a, h, way, s]

    y_last, z_last = [None] * 3, [[None, None], [None, None]]

    def y_step(n, s):
        y_last[n] = reduce_step(y_buf, y_ss, y_rs, (y_up, y_down), WSTEPS[n], n, s, y_last[n], own_w)

    def y_end(n):
        return reduce_end(y_buf, WSTEPS[n], n, y_last[n], own_w)

    def z_step(a, s, halves=(0, 1)):
        for h in halves:
            z_last[a][h] = reduce_step(
                z_buf(a), z_ss.at[a], z_rs.at[a], (up, down), STEPS[h], h, s, z_last[a][h], own_part(a)
            )

    def combine(a, weights, moves, begin=0, width=D):
        for move in moves:
            move.wait_recv()

        def summed(cols):
            part[a, :, cols] = nn(weights[...], recv_x[2 + a, :, cols])

        def step(i, carry):
            summed(pl.ds(pl.multiple_of(begin + i * WIDE, WIDE), WIDE))
            return carry

        lax.fori_loop(0, width // WIDE, step, 0)

    def z_end(a, h, result):
        total = reduce_end(z_buf(a), STEPS[h], h, z_last[a][h], own_part(a))
        result[:, h * HALF : (h + 1) * HALF] = total.astype(BF)

    def backward(cols):
        da = nt(recv_x[1], wd_ref[cols, :])
        dpre[:, cols] = (da * keep_d[:, cols]).astype(BF)
        dpre[:, pl.ds(pl.multiple_of(cols.start + FF, WIDE), WIDE)] = (da * keep_s[:, cols]).astype(BF)

    def backward_in(cols):
        both = nt(dpre[:, 0:FF], wg_ref[cols, :]) + nt(dpre[:, FF : 2 * FF], wu_ref[cols, :])
        send_x[3, :, cols] = both.astype(BF)

    chunks(D // WIDE, weight_down)
    y_step(2, 1)
    chunks(FF // WIDE, backward)
    chunks(D // WIDE, backward_in)
    grad_moves = [exchange(3, -1, h * HALF, HALF) for h in range(2)]
    chunks(2 * FF // WIDE, weight_both)
    y_step(0, 1)
    y_step(1, 1)
    y_step(2, 2)
    combine(0, pickg_t, out_moves)
    z_step(0, 1)
    y_step(0, 2)
    y_step(1, 2)
    z_step(0, 2)
    y_step(2, 3)
    z_step(0, 3)
    combine(1, pick_t, grad_moves[0], 0, HALF)
    z_step(1, 1, (0,))
    y_step(0, 3)
    z_step(0, 4)
    y_step(1, 3)
    z_step(1, 2, (0,))
    for h in range(2):
        z_end(0, h, out_ref)
    y_step(2, 4)
    z_step(1, 3, (0,))
    combine(1, pick_t, grad_moves[1], HALF, HALF)
    z_step(1, 1, (1,))
    z_step(1, 4, (0,))
    y_step(0, 4)
    z_step(1, 2, (1,))
    y_step(1, 4)
    z_step(1, 3, (1,))
    z_end(1, 0, dtok_ref)
    dd_ref[...] = y_end(2)
    z_step(1, 4, (1,))
    dg_ref[...] = y_end(0)
    du_ref[...] = y_end(1)
    z_end(1, 1, dtok_ref)

    for copy in started:
        copy.wait_send()


def place(*refs):
    for src, dst in zip(refs[:5], refs[5:]):
        dst[...] = src[...]


def on_device(tokens, expert_ids, gate_values, cotangent, w_gate, w_up, w_down):
    vmem = pl.BlockSpec(memory_space=pltpu.VMEM)
    hbm = pl.BlockSpec(memory_space=pl.ANY)
    dma = pltpu.SemaphoreType.DMA
    shapes = (
        jax.ShapeDtypeStruct((TOK, D), BF),
        jax.ShapeDtypeStruct((TOK, D), BF),
        jax.ShapeDtypeStruct((128, FF), F32),
        jax.ShapeDtypeStruct((128, FF), F32),
        jax.ShapeDtypeStruct((FF, 128), F32),
    )
    results = pl.pallas_call(
        kernel,
        out_shape=shapes,
        in_specs=[vmem] * 4 + [hbm] * 3,
        out_specs=(vmem,) * 5,
        scratch_shapes=[
            pltpu.VMEM((NZ, TOK, 2 * EXPERTS), BF),
            pltpu.VMEM((2, 2, NZ, TOK, HALF), BF),
            pltpu.VMEM((ROWS, GATHERED), BF),
            pltpu.VMEM((GATHERED, ROWS), BF),
            pltpu.VMEM((GATHERED, ROWS), BF),
            pltpu.VMEM((ROWS, 128), F32),
            pltpu.VMEM((4, ROWS, D), BF),
            pltpu.VMEM((4, ROWS, D), BF),
            pltpu.VMEM((ROWS, FF), F32),
            pltpu.VMEM((ROWS, FF), F32),
            pltpu.VMEM((ROWS, FF), BF),
            pltpu.VMEM((ROWS, 2 * FF), BF),
            pltpu.VMEM((2, GATHERED, D), F32),
            pltpu.VMEM((2, 2, 2, 5, TOK, HALF), BF),
            pltpu.VMEM((D, 2 * FF), F32),
            pltpu.VMEM((FF, D), F32),
            pltpu.VMEM((2, 2, 5, 128, FF), BF),
            pltpu.VMEM((2, 5, FF, 128), BF),
            pltpu.VMEM((FF, ROWS), BF),
            pltpu.VMEM((D, ROWS), BF),
            pltpu.VMEM((D, FF), BF),
            pltpu.VMEM((D, FF), BF),
            pltpu.VMEM((FF, D), BF),
            dma((NZ,)), dma((NZ,)),
            dma((2, 2, NZ)), dma((2, 2, NZ)),
            dma((5, PEERS)), dma((5, PEERS)),
            dma((2, 2, 2, 5)), dma((2, 2, 2, 5)),
            dma((3, 2, 5)), dma((3, 2, 5)),
            dma((3,)),
        ],
        compiler_params=pltpu.CompilerParams(
            collective_id=0, has_side_effects=True, vmem_limit_bytes=58 * 1024 * 1024
        ),
        cost_estimate=pl.CostEstimate(flops=7_000_000_000, bytes_accessed=8_000_000, transcendentals=400_000),
    )(expert_ids.T, gate_values.T, tokens, cotangent, w_gate[0], w_up[0], w_down[0])
    out, dtok, dg, du, dd = pl.pallas_call(
        place,
        out_shape=shapes,
        in_specs=[vmem] * 5,
        out_specs=(vmem,) * 5,
    )(*results)
    return out, dtok, dg[None], du[None], dd[None]


def solution(mesh):
    rows = P(("dp", "expert"), None)
    weights = P("expert", None, None)
    return jax.shard_map(
        on_device,
        mesh=mesh,
        in_specs=(rows,) * 4 + (weights,) * 3,
        out_specs=(rows, rows, P("expert", "dp", None), P("expert", "dp", None), P("expert", None, "dp")),
        check_vma=False,
    )
```

```python
import jax
import jax.numpy as jnp
from jax import lax
from jax.experimental import pallas as pl
from jax.experimental.pallas import tpu as pltpu
from jax.sharding import PartitionSpec as P

MESH = pl.DeviceIdType.MESH
BF = jnp.bfloat16
F32 = jnp.float32
NX, NZ, NC = 4, 8, 2
NY = 8
TOK = 64
D = 1024
HALF = D // 2
FF = 512
CAP = 10
SLOTS = NZ * CAP
PEERS = NX * NC
ROWS = PEERS * SLOTS
GATHERED = NZ * TOK
EXPERTS = NX * NZ * NC
WIDE = 256
STEPS = ((4, 3), (3, 4))
WSTEPS = ((3, 4), (4, 3), (4, 3))


def nn(a, b):
    return jnp.dot(a, b, preferred_element_type=F32)


def nt(a, b):
    return lax.dot_general(a, b, (((1,), (1,)), ((), ())), preferred_element_type=F32)


def tn(a, b):
    return lax.dot_general(a, b, (((0,), (0,)), ((), ())), preferred_element_type=F32)


def kernel(
    ids_ref, gv_ref, tok_ref, cot_ref, wg_hbm, wu_hbm, wd_hbm,
    out_ref, dtok_ref, dg_ref, du_ref, dd_ref,
    meta, gath, pick, pick_t, pickg_t, gslot, send_x, recv_x, keep_s, keep_d, act, dpre, part, zbuf, wboth, wdown, yboth, ydown, act_t, tok_t, wg_ref, wu_ref, wd_ref,
    m_ss, m_rs, g_ss, g_rs, x_ss, x_rs, z_ss, z_rs, y_ss, y_rs, w_s,
):
    y = lax.axis_index("dp")
    e = lax.axis_index("expert")
    c = e % 2
    z = (e // 2) % NZ
    x = e // (2 * NZ)
    up = (y, (x * NZ + (z + 1) % NZ) * 2 + c)
    down = (y, (x * NZ + (z + NZ - 1) % NZ) * 2 + c)
    y_up = ((y + 1) % NY, e)
    y_down = ((y + NY - 1) % NY, e)

    def peer(j, sign):
        dx, dc = j // 2, j % 2
        return (y, (((x + sign * dx + NX) % NX) * NZ + z) * 2 + (c + dc) % 2)

    loads = [
        pltpu.make_async_copy(src, dst, w_s.at[n])
        for n, (src, dst) in enumerate(((wg_hbm, wg_ref), (wu_hbm, wu_ref), (wd_hbm, wd_ref)))
    ]
    for load in loads:
        load.start()
    barrier = pltpu.get_barrier_semaphore()
    friends = [up, down, y_up, y_down] + [peer(j, 1) for j in range(1, PEERS)]
    for friend in friends:
        pl.semaphore_signal(barrier, inc=1, device_id=friend, device_id_type=MESH)

    line = lax.broadcasted_iota(jnp.int32, (2 * EXPERTS, TOK), 0)
    gate = jnp.zeros((2 * EXPERTS, TOK), F32)
    for k in range(8):
        gate = jnp.where(line % EXPERTS == ids_ref[k : k + 1, :], gv_ref[k : k + 1, :], gate)
    gate = gate.T
    lane = lax.broadcasted_iota(jnp.int32, (TOK, 2 * EXPERTS), 1)
    high = gate.astype(BF).astype(F32)
    meta[0] = jnp.where(lane < EXPERTS, high, gate - high).astype(BF)
    for h in range(2):
        gath[0, h, 0] = tok_ref[:, h * HALF : (h + 1) * HALF]
        gath[1, h, 0] = cot_ref[:, h * HALF : (h + 1) * HALF]

    pl.semaphore_wait(barrier, len(friends))

    started = []

    def send(src, dst, ss, rs, to):
        copy = pltpu.make_async_remote_copy(
            src_ref=src, dst_ref=dst, send_sem=ss, recv_sem=rs, device_id=to, device_id_type=MESH
        )
        copy.start()
        started.append(copy)
        return copy

    def gather_step(buf, ss, rs, steps, s, prev):
        now = []
        for way, (to, count) in enumerate(zip((up, down), steps)):
            if s > count:
                now.append(None)
                continue
            if s > 1:
                prev[way].wait_recv()
            src = (NZ - s + 1) % NZ if way == 0 else s - 1
            dst = NZ - s if way == 0 else s
            now.append(send(buf.at[src], buf.at[dst], ss.at[dst], rs.at[dst], to))
        return [n if n is not None else p for n, p in zip(now, prev or (None, None))]

    m_last, t_last, c_last = None, [None, None], [None, None]
    for s in range(1, 5):
        m_last = gather_step(meta, m_ss, m_rs, STEPS[0], s, m_last)
        for h in range(2):
            t_last[h] = gather_step(gath.at[0, h], g_ss.at[0, h], g_rs.at[0, h], STEPS[h], s, t_last[h])
    for h in range(2):
        c_last[h] = gather_step(gath.at[1, h], g_ss.at[1, h], g_rs.at[1, h], STEPS[h], 1, None)

    for way in range(2):
        m_last[way].wait_recv()
    row = lax.broadcasted_iota(jnp.int32, (16, 2 * EXPERTS), 0)
    col = lax.broadcasted_iota(jnp.int32, (16, 2 * EXPERTS), 1)
    wanted = (((x + (row % PEERS) // 2) % NX) * NZ + z) * 2 + (c + row) % 2
    chosen = jnp.where(col % EXPERTS == wanted, 1.0, 0.0).astype(BF)
    gate_row = nt(chosen, meta[...].reshape(GATHERED, 2 * EXPERTS))
    match = jnp.where(gate_row > 0.0, 1.0, 0.0)
    first = lax.broadcasted_iota(jnp.int32, (GATHERED, GATHERED), 0)
    second = lax.broadcasted_iota(jnp.int32, (GATHERED, GATHERED), 1)
    rank = nn(match.astype(BF), jnp.where(first < second, 1.0, 0.0).astype(BF))
    place = jnp.where(gate_row > 0.0, rank, -1.0)
    slot = lax.broadcasted_iota(jnp.int32, (SLOTS, GATHERED), 0).astype(F32)
    for j in range(PEERS):
        hit = slot == place[j : j + 1, :]
        pick[j * SLOTS : (j + 1) * SLOTS, :] = jnp.where(hit, 1.0, 0.0).astype(BF)
        weight = jnp.sum(jnp.where(hit, gate_row[j : j + 1, :], 0.0), axis=1, keepdims=True)
        gslot[j * SLOTS : (j + 1) * SLOTS, :] = jnp.broadcast_to(weight, (SLOTS, 128))

    for h in range(2):
        for way in range(2):
            t_last[h][way].wait_recv()

    def chunks(count, body):
        def step(i, carry):
            body(pl.ds(pl.multiple_of(i * WIDE, WIDE), WIDE))
            return carry

        lax.fori_loop(0, count, step, 0)

    def exchange(n, sign, begin=0, width=D):
        sem = 4 if begin else n
        cols = pl.ds(begin, width)
        recv_x[n, 0:SLOTS, cols] = send_x[n, 0:SLOTS, cols]
        copies = []
        for j in (4, 5, 2, 3, 6, 7, 1):
            block = pl.ds(j * SLOTS, SLOTS)
            src, dst = send_x.at[n, block, cols], recv_x.at[n, block, cols]
            copies.append(send(src, dst, x_ss.at[sem, j], x_rs.at[sem, j], peer(j, sign)))
        return copies

    def picked(a, h):
        source = gath[a, h].reshape(GATHERED, HALF)
        return nn(pick[...], source)

    for h in range(2):
        send_x[0, :, h * HALF : (h + 1) * HALF] = picked(0, h).astype(BF)
    tok_moves = exchange(0, 1)

    for s in range(2, 5):
        for h in range(2):
            c_last[h] = gather_step(gath.at[1, h], g_ss.at[1, h], g_rs.at[1, h], STEPS[h], s, c_last[h])
    for h in range(2):
        for way in range(2):
            c_last[h][way].wait_recv()

    for h in range(2):
        send_x[1, :, h * HALF : (h + 1) * HALF] = (picked(1, h) * gslot[:, 0:1]).astype(BF)
    cot_moves = exchange(1, 1)

    for q in range(4):
        cols = slice(q * 128, (q + 1) * 128)
        plain = pick[:, cols].astype(F32)
        pick_t[cols, :] = plain.T.astype(BF)
        pickg_t[cols, :] = (plain * gslot[...]).T.astype(BF)

    for load in loads:
        load.wait()
    for move in tok_moves:
        move.wait_recv()

    def forward(cols):
        g = nn(recv_x[0], wg_ref[:, cols])
        u = nn(recv_x[0], wu_ref[:, cols])
        s = jax.nn.sigmoid(g)
        silu = g * s
        keep_s[:, cols] = silu
        keep_d[:, cols] = u * s * (1.0 + g * (1.0 - s))
        act[:, cols] = (silu * u).astype(BF)

    def forward_out(cols):
        send_x[2, :, cols] = nn(act[...], wd_ref[:, cols]).astype(BF)

    chunks(FF // WIDE, forward)
    chunks(D // WIDE, forward_out)
    out_moves = exchange(2, -1)
    for q in range(FF // 128):
        act_t[q * 128 : (q + 1) * 128, :] = act[:, q * 128 : (q + 1) * 128].astype(F32).T.astype(BF)
    for q in range(D // 128):
        tok_t[q * 128 : (q + 1) * 128, :] = recv_x[0, :, q * 128 : (q + 1) * 128].astype(F32).T.astype(BF)
    for move in cot_moves:
        move.wait_recv()

    def weight_down(cols):
        wdown[:, cols] = nn(act_t[...], recv_x[1, :, cols])

    def weight_both(cols):
        wboth[:, cols] = nn(tok_t[...], dpre[:, cols])

    def reduce_step(buf, ss, rs, ways, steps, h, s, prev, own):
        now = []
        for way in range(2):
            count = steps[way]
            if s > count:
                now.append(prev[way])
                continue
            ahead = count + 1 - s
            term = own(ahead if way == 0 else 8 - ahead, h)
            if s > 1:
                prev[way].wait_recv()
                term = term + buf(h, way, s - 1)[...].astype(F32)
            buf(h, way, s - 1)[...] = term.astype(BF)
            now.append(
                send(buf(h, way, s - 1), buf(h, way, s), ss.at[h, way, s], rs.at[h, way, s], ways[way])
            )
        return now

    def reduce_end(buf, steps, h, prev, own):
        for way in range(2):
            prev[way].wait_recv()
        first, second = steps
        return own(0, h) + buf(h, 0, first)[...].astype(F32) + buf(h, 1, second)[...].astype(F32)

    def own_w(k, n):
        there = pl.ds(pl.multiple_of(((y + k) % NY) * 128, 128), 128)
        if n == 2:
            return wdown[:, there]
        return wboth[there, n * FF : (n + 1) * FF]

    def own_part(a):
        return lambda k, h: part[a, k * TOK : (k + 1) * TOK, h * HALF : (h + 1) * HALF]

    def y_buf(n, way, s):
        return ydown.at[way, s] if n == 2 else yboth.at[n, way, s]

    def z_buf(a):
        return lambda h, way, s: zbuf.at[a, h, way, s]

    y_last, z_last = [None] * 3, [[None, None], [None, None]]

    def y_step(n, s):
        y_last[n] = reduce_step(y_buf, y_ss, y_rs, (y_up, y_down), WSTEPS[n], n, s, y_last[n], own_w)

    def y_end(n):
        return reduce_end(y_buf, WSTEPS[n], n, y_last[n], own_w)

    def z_step(a, s, halves=(0, 1)):
        for h in halves:
            z_last[a][h] = reduce_step(
                z_buf(a), z_ss.at[a], z_rs.at[a], (up, down), STEPS[h], h, s, z_last[a][h], own_part(a)
            )

    def combine(a, weights, moves, begin=0, width=D):
        for move in moves:
            move.wait_recv()

        def summed(cols):
            part[a, :, cols] = nn(weights[...], recv_x[2 + a, :, cols])

        def step(i, carry):
            summed(pl.ds(pl.multiple_of(begin + i * WIDE, WIDE), WIDE))
            return carry

        lax.fori_loop(0, width // WIDE, step, 0)

    def z_end(a, h, result):
        total = reduce_end(z_buf(a), STEPS[h], h, z_last[a][h], own_part(a))
        result[:, h * HALF : (h + 1) * HALF] = total.astype(BF)

    def backward(cols):
        da = nt(recv_x[1], wd_ref[cols, :])
        dpre[:, cols] = (da * keep_d[:, cols]).astype(BF)
        dpre[:, pl.ds(pl.multiple_of(cols.start + FF, WIDE), WIDE)] = (da * keep_s[:, cols]).astype(BF)

    def backward_in(cols):
        both = nt(dpre[:, 0:FF], wg_ref[cols, :]) + nt(dpre[:, FF : 2 * FF], wu_ref[cols, :])
        send_x[3, :, cols] = both.astype(BF)

    chunks(D // WIDE, weight_down)
    y_step(2, 1)
    chunks(FF // WIDE, backward)
    chunks(D // WIDE, backward_in)
    grad_moves = [exchange(3, -1, h * HALF, HALF) for h in range(2)]
    chunks(2 * FF // WIDE, weight_both)
    y_step(0, 1)
    y_step(1, 1)
    y_step(2, 2)
    combine(0, pickg_t, out_moves)
    z_step(0, 1)
    y_step(0, 2)
    y_step(1, 2)
    z_step(0, 2)
    combine(1, pick_t, grad_moves[0], 0 * HALF, HALF)
    z_step(1, 1, (0,))
    y_step(2, 3)
    z_step(0, 3)
    z_step(1, 2, (0,))
    combine(1, pick_t, grad_moves[1], 1 * HALF, HALF)
    z_step(1, 1, (1,))
    z_step(0, 4)
    z_step(1, 3, (0,))
    y_step(0, 3)
    z_step(1, 2, (1,))
    y_step(1, 3)
    for h in range(2):
        z_end(0, h, out_ref)
    z_step(1, 4, (0,))
    y_step(2, 4)
    z_step(1, 3, (1,))
    y_step(0, 4)
    z_step(1, 4, (1,))
    y_step(1, 4)
    z_end(1, 0, dtok_ref)
    dd_ref[...] = y_end(2)
    dg_ref[...] = y_end(0)
    z_end(1, 1, dtok_ref)
    du_ref[...] = y_end(1)

    for copy in started:
        copy.wait_send()


def place(*refs):
    for src, dst in zip(refs[:5], refs[5:]):
        dst[...] = src[...]


def on_device(tokens, expert_ids, gate_values, cotangent, w_gate, w_up, w_down):
    vmem = pl.BlockSpec(memory_space=pltpu.VMEM)
    hbm = pl.BlockSpec(memory_space=pl.ANY)
    dma = pltpu.SemaphoreType.DMA
    shapes = (
        jax.ShapeDtypeStruct((TOK, D), BF),
        jax.ShapeDtypeStruct((TOK, D), BF),
        jax.ShapeDtypeStruct((128, FF), F32),
        jax.ShapeDtypeStruct((128, FF), F32),
        jax.ShapeDtypeStruct((FF, 128), F32),
    )
    results = pl.pallas_call(
        kernel,
        out_shape=shapes,
        in_specs=[vmem] * 4 + [hbm] * 3,
        out_specs=(vmem,) * 5,
        scratch_shapes=[
            pltpu.VMEM((NZ, TOK, 2 * EXPERTS), BF),
            pltpu.VMEM((2, 2, NZ, TOK, HALF), BF),
            pltpu.VMEM((ROWS, GATHERED), BF),
            pltpu.VMEM((GATHERED, ROWS), BF),
            pltpu.VMEM((GATHERED, ROWS), BF),
            pltpu.VMEM((ROWS, 128), F32),
            pltpu.VMEM((4, ROWS, D), BF),
            pltpu.VMEM((4, ROWS, D), BF),
            pltpu.VMEM((ROWS, FF), F32),
            pltpu.VMEM((ROWS, FF), F32),
            pltpu.VMEM((ROWS, FF), BF),
            pltpu.VMEM((ROWS, 2 * FF), BF),
            pltpu.VMEM((2, GATHERED, D), F32),
            pltpu.VMEM((2, 2, 2, 5, TOK, HALF), BF),
            pltpu.VMEM((D, 2 * FF), F32),
            pltpu.VMEM((FF, D), F32),
            pltpu.VMEM((2, 2, 5, 128, FF), BF),
            pltpu.VMEM((2, 5, FF, 128), BF),
            pltpu.VMEM((FF, ROWS), BF),
            pltpu.VMEM((D, ROWS), BF),
            pltpu.VMEM((D, FF), BF),
            pltpu.VMEM((D, FF), BF),
            pltpu.VMEM((FF, D), BF),
            dma((NZ,)), dma((NZ,)),
            dma((2, 2, NZ)), dma((2, 2, NZ)),
            dma((5, PEERS)), dma((5, PEERS)),
            dma((2, 2, 2, 5)), dma((2, 2, 2, 5)),
            dma((3, 2, 5)), dma((3, 2, 5)),
            dma((3,)),
        ],
        compiler_params=pltpu.CompilerParams(
            collective_id=0, has_side_effects=True, vmem_limit_bytes=58 * 1024 * 1024
        ),
        cost_estimate=pl.CostEstimate(flops=7_000_000_000, bytes_accessed=8_000_000, transcendentals=400_000),
    )(expert_ids.T, gate_values.T, tokens, cotangent, w_gate[0], w_up[0], w_down[0])
    out, dtok, dg, du, dd = pl.pallas_call(
        place,
        out_shape=shapes,
        in_specs=[vmem] * 5,
        out_specs=(vmem,) * 5,
    )(*results)
    return out, dtok, dg[None], du[None], dd[None]


def solution(mesh):
    rows = P(("dp", "expert"), None)
    weights = P("expert", None, None)
    return jax.shard_map(
        on_device,
        mesh=mesh,
        in_specs=(rows,) * 4 + (weights,) * 3,
        out_specs=(rows, rows, P("expert", "dp", None), P("expert", "dp", None), P("expert", None, "dp")),
        check_vma=False,
    )
```

```python
import jax
import jax.numpy as jnp
from jax import lax
from jax.experimental import pallas as pl
from jax.experimental.pallas import tpu as pltpu
from jax.sharding import PartitionSpec as P

MESH = pl.DeviceIdType.MESH
BF = jnp.bfloat16
F32 = jnp.float32
NX, NZ, NC = 4, 8, 2
NY = 8
TOK = 64
D = 1024
HALF = D // 2
FF = 512
CAP = 10
SLOTS = NZ * CAP
PEERS = NX * NC
ROWS = PEERS * SLOTS
GATHERED = NZ * TOK
EXPERTS = NX * NZ * NC
WIDE = 256
STEPS = ((4, 3), (3, 4))
WSTEPS = ((3, 4), (4, 3), (4, 3))


def nn(a, b):
    return jnp.dot(a, b, preferred_element_type=F32)


def nt(a, b):
    return lax.dot_general(a, b, (((1,), (1,)), ((), ())), preferred_element_type=F32)


def tn(a, b):
    return lax.dot_general(a, b, (((0,), (0,)), ((), ())), preferred_element_type=F32)


def kernel(
    ids_ref, gv_ref, tok_ref, cot_ref, wg_hbm, wu_hbm, wd_hbm,
    out_ref, dtok_ref, dg_ref, du_ref, dd_ref,
    meta, gath, pick, pick_t, pickg_t, gslot, send_x, recv_x, keep_s, keep_d, act, dpre, part, zbuf, wboth, wdown, yboth, ydown, act_t, tok_t, wg_ref, wu_ref, wd_ref,
    m_ss, m_rs, g_ss, g_rs, x_ss, x_rs, z_ss, z_rs, y_ss, y_rs, w_s,
):
    y = lax.axis_index("dp")
    e = lax.axis_index("expert")
    c = e % 2
    z = (e // 2) % NZ
    x = e // (2 * NZ)
    up = (y, (x * NZ + (z + 1) % NZ) * 2 + c)
    down = (y, (x * NZ + (z + NZ - 1) % NZ) * 2 + c)
    y_up = ((y + 1) % NY, e)
    y_down = ((y + NY - 1) % NY, e)

    def peer(j, sign):
        dx, dc = j // 2, j % 2
        return (y, (((x + sign * dx + NX) % NX) * NZ + z) * 2 + (c + dc) % 2)

    loads = [
        pltpu.make_async_copy(src, dst, w_s.at[n])
        for n, (src, dst) in enumerate(((wg_hbm, wg_ref), (wu_hbm, wu_ref), (wd_hbm, wd_ref)))
    ]
    for load in loads:
        load.start()
    barrier = pltpu.get_barrier_semaphore()
    friends = [up, down, y_up, y_down] + [peer(j, 1) for j in range(1, PEERS)]
    for friend in friends:
        pl.semaphore_signal(barrier, inc=1, device_id=friend, device_id_type=MESH)

    line = lax.broadcasted_iota(jnp.int32, (2 * EXPERTS, TOK), 0)
    gate = jnp.zeros((2 * EXPERTS, TOK), F32)
    for k in range(8):
        gate = jnp.where(line % EXPERTS == ids_ref[k : k + 1, :], gv_ref[k : k + 1, :], gate)
    gate = gate.T
    lane = lax.broadcasted_iota(jnp.int32, (TOK, 2 * EXPERTS), 1)
    high = gate.astype(BF).astype(F32)
    meta[0] = jnp.where(lane < EXPERTS, high, gate - high).astype(BF)
    for h in range(2):
        gath[0, h, 0] = tok_ref[:, h * HALF : (h + 1) * HALF]
        gath[1, h, 0] = cot_ref[:, h * HALF : (h + 1) * HALF]

    pl.semaphore_wait(barrier, len(friends))

    started = []

    def send(src, dst, ss, rs, to):
        copy = pltpu.make_async_remote_copy(
            src_ref=src, dst_ref=dst, send_sem=ss, recv_sem=rs, device_id=to, device_id_type=MESH
        )
        copy.start()
        started.append(copy)
        return copy

    def gather_step(buf, ss, rs, steps, s, prev):
        now = []
        for way, (to, count) in enumerate(zip((up, down), steps)):
            if s > count:
                now.append(None)
                continue
            if s > 1:
                prev[way].wait_recv()
            src = (NZ - s + 1) % NZ if way == 0 else s - 1
            dst = NZ - s if way == 0 else s
            now.append(send(buf.at[src], buf.at[dst], ss.at[dst], rs.at[dst], to))
        return [n if n is not None else p for n, p in zip(now, prev or (None, None))]

    m_last, t_last, c_last = None, [None, None], [None, None]
    for s in range(1, 5):
        m_last = gather_step(meta, m_ss, m_rs, STEPS[0], s, m_last)
        for h in range(2):
            t_last[h] = gather_step(gath.at[0, h], g_ss.at[0, h], g_rs.at[0, h], STEPS[h], s, t_last[h])
    for h in range(2):
        c_last[h] = gather_step(gath.at[1, h], g_ss.at[1, h], g_rs.at[1, h], STEPS[h], 1, None)

    for way in range(2):
        m_last[way].wait_recv()
    row = lax.broadcasted_iota(jnp.int32, (16, 2 * EXPERTS), 0)
    col = lax.broadcasted_iota(jnp.int32, (16, 2 * EXPERTS), 1)
    wanted = (((x + (row % PEERS) // 2) % NX) * NZ + z) * 2 + (c + row) % 2
    chosen = jnp.where(col % EXPERTS == wanted, 1.0, 0.0).astype(BF)
    gate_row = nt(chosen, meta[...].reshape(GATHERED, 2 * EXPERTS))
    match = jnp.where(gate_row > 0.0, 1.0, 0.0)
    first = lax.broadcasted_iota(jnp.int32, (GATHERED, GATHERED), 0)
    second = lax.broadcasted_iota(jnp.int32, (GATHERED, GATHERED), 1)
    rank = nn(match.astype(BF), jnp.where(first < second, 1.0, 0.0).astype(BF))
    place = jnp.where(gate_row > 0.0, rank, -1.0)
    slot = lax.broadcasted_iota(jnp.int32, (SLOTS, GATHERED), 0).astype(F32)
    for j in range(PEERS):
        hit = slot == place[j : j + 1, :]
        pick[j * SLOTS : (j + 1) * SLOTS, :] = jnp.where(hit, 1.0, 0.0).astype(BF)

    def chunks(count, body):
        def step(i, carry):
            body(pl.ds(pl.multiple_of(i * WIDE, WIDE), WIDE))
            return carry

        lax.fori_loop(0, count, step, 0)

    def exchange(n, sign, begin=0, width=D):
        sem = 2 * n + (begin > 0)
        cols = pl.ds(begin, width)
        recv_x[n, 0:SLOTS, cols] = send_x[n, 0:SLOTS, cols]
        copies = []
        for j in (4, 5, 2, 3, 6, 7, 1):
            block = pl.ds(j * SLOTS, SLOTS)
            src, dst = send_x.at[n, block, cols], recv_x.at[n, block, cols]
            copies.append(send(src, dst, x_ss.at[sem, j], x_rs.at[sem, j], peer(j, sign)))
        return copies

    def picked(a, h):
        source = gath[a, h].reshape(GATHERED, HALF)
        return nn(pick[...], source)

    tok_moves = []
    for h in range(2):
        for way in range(2):
            t_last[h][way].wait_recv()
        send_x[0, :, h * HALF : (h + 1) * HALF] = picked(0, h).astype(BF)
        tok_moves += exchange(0, 1, h * HALF, HALF)
    for j in range(PEERS):
        hit = slot == place[j : j + 1, :]
        weight = jnp.sum(jnp.where(hit, gate_row[j : j + 1, :], 0.0), axis=1, keepdims=True)
        gslot[j * SLOTS : (j + 1) * SLOTS, :] = jnp.broadcast_to(weight, (SLOTS, 128))

    for s in range(2, 5):
        for h in range(2):
            c_last[h] = gather_step(gath.at[1, h], g_ss.at[1, h], g_rs.at[1, h], STEPS[h], s, c_last[h])
    cot_moves = []
    for h in range(2):
        for way in range(2):
            c_last[h][way].wait_recv()
        send_x[1, :, h * HALF : (h + 1) * HALF] = (picked(1, h) * gslot[:, 0:1]).astype(BF)
        cot_moves += exchange(1, 1, h * HALF, HALF)

    for q in range(4):
        cols = slice(q * 128, (q + 1) * 128)
        plain = pick[:, cols].astype(F32)
        pick_t[cols, :] = plain.T.astype(BF)
        pickg_t[cols, :] = (plain * gslot[...]).T.astype(BF)

    for load in loads:
        load.wait()
    for move in tok_moves:
        move.wait_recv()

    def forward(cols):
        g = nn(recv_x[0], wg_ref[:, cols])
        u = nn(recv_x[0], wu_ref[:, cols])
        s = jax.nn.sigmoid(g)
        silu = g * s
        keep_s[:, cols] = silu
        keep_d[:, cols] = u * s * (1.0 + g * (1.0 - s))
        act[:, cols] = (silu * u).astype(BF)

    def forward_out(cols):
        send_x[2, :, cols] = nn(act[...], wd_ref[:, cols]).astype(BF)

    chunks(FF // WIDE, forward)
    chunks(D // WIDE, forward_out)
    out_moves = exchange(2, -1)
    for q in range(FF // 128):
        act_t[q * 128 : (q + 1) * 128, :] = act[:, q * 128 : (q + 1) * 128].astype(F32).T.astype(BF)
    for q in range(D // 128):
        tok_t[q * 128 : (q + 1) * 128, :] = recv_x[0, :, q * 128 : (q + 1) * 128].astype(F32).T.astype(BF)
    for move in cot_moves:
        move.wait_recv()

    def weight_down(cols):
        wdown[:, cols] = nn(act_t[...], recv_x[1, :, cols])

    def weight_both(cols):
        wboth[:, cols] = nn(tok_t[...], dpre[:, cols])

    def reduce_step(buf, ss, rs, ways, steps, h, s, prev, own):
        now = []
        for way in range(2):
            count = steps[way]
            if s > count:
                now.append(prev[way])
                continue
            ahead = count + 1 - s
            term = own(ahead if way == 0 else 8 - ahead, h)
            if s > 1:
                prev[way].wait_recv()
                term = term + buf(h, way, s - 1)[...].astype(F32)
            buf(h, way, s - 1)[...] = term.astype(BF)
            now.append(
                send(buf(h, way, s - 1), buf(h, way, s), ss.at[h, way, s], rs.at[h, way, s], ways[way])
            )
        return now

    def reduce_end(buf, steps, h, prev, own):
        for way in range(2):
            prev[way].wait_recv()
        first, second = steps
        return own(0, h) + buf(h, 0, first)[...].astype(F32) + buf(h, 1, second)[...].astype(F32)

    def own_w(k, n):
        there = pl.ds(pl.multiple_of(((y + k) % NY) * 128, 128), 128)
        if n == 2:
            return wdown[:, there]
        return wboth[there, n * FF : (n + 1) * FF]

    def own_part(a):
        return lambda k, h: part[a, k * TOK : (k + 1) * TOK, h * HALF : (h + 1) * HALF]

    def y_buf(n, way, s):
        return ydown.at[way, s] if n == 2 else yboth.at[n, way, s]

    def z_buf(a):
        return lambda h, way, s: zbuf.at[a, h, way, s]

    y_last, z_last = [None] * 3, [[None, None], [None, None]]

    def y_step(n, s):
        y_last[n] = reduce_step(y_buf, y_ss, y_rs, (y_up, y_down), WSTEPS[n], n, s, y_last[n], own_w)

    def y_end(n):
        return reduce_end(y_buf, WSTEPS[n], n, y_last[n], own_w)

    def z_step(a, s, halves=(0, 1)):
        for h in halves:
            z_last[a][h] = reduce_step(
                z_buf(a), z_ss.at[a], z_rs.at[a], (up, down), STEPS[h], h, s, z_last[a][h], own_part(a)
            )

    def combine(a, weights, moves, begin=0, width=D):
        for move in moves:
            move.wait_recv()

        def summed(cols):
            part[a, :, cols] = nn(weights[...], recv_x[2 + a, :, cols])

        def step(i, carry):
            summed(pl.ds(pl.multiple_of(begin + i * WIDE, WIDE), WIDE))
            return carry

        lax.fori_loop(0, width // WIDE, step, 0)

    def z_end(a, h, result):
        total = reduce_end(z_buf(a), STEPS[h], h, z_last[a][h], own_part(a))
        result[:, h * HALF : (h + 1) * HALF] = total.astype(BF)

    def backward(cols):
        da = nt(recv_x[1], wd_ref[cols, :])
        dpre[:, cols] = (da * keep_d[:, cols]).astype(BF)
        dpre[:, pl.ds(pl.multiple_of(cols.start + FF, WIDE), WIDE)] = (da * keep_s[:, cols]).astype(BF)

    def backward_in(cols):
        both = nt(dpre[:, 0:FF], wg_ref[cols, :]) + nt(dpre[:, FF : 2 * FF], wu_ref[cols, :])
        send_x[3, :, cols] = both.astype(BF)

    chunks(D // WIDE, weight_down)
    y_step(2, 1)
    chunks(FF // WIDE, backward)
    chunks(D // WIDE, backward_in)
    grad_moves = [exchange(3, -1, h * HALF, HALF) for h in range(2)]
    chunks(2 * FF // WIDE, weight_both)
    y_step(0, 1)
    y_step(1, 1)
    y_step(2, 2)
    combine(0, pickg_t, out_moves)
    z_step(0, 1)
    y_step(0, 2)
    y_step(1, 2)
    z_step(0, 2)
    combine(1, pick_t, grad_moves[0], 0 * HALF, HALF)
    z_step(1, 1, (0,))
    y_step(2, 3)
    z_step(0, 3)
    z_step(1, 2, (0,))
    combine(1, pick_t, grad_moves[1], 1 * HALF, HALF)
    z_step(1, 1, (1,))
    z_step(0, 4)
    z_step(1, 3, (0,))
    y_step(0, 3)
    z_step(1, 2, (1,))
    y_step(1, 3)
    for h in range(2):
        z_end(0, h, out_ref)
    z_step(1, 4, (0,))
    y_step(2, 4)
    z_step(1, 3, (1,))
    y_step(0, 4)
    z_step(1, 4, (1,))
    y_step(1, 4)
    z_end(1, 0, dtok_ref)
    dd_ref[...] = y_end(2)
    dg_ref[...] = y_end(0)
    z_end(1, 1, dtok_ref)
    du_ref[...] = y_end(1)

    for copy in started:
        copy.wait_send()


def place(*refs):
    for src, dst in zip(refs[:5], refs[5:]):
        dst[...] = src[...]


def on_device(tokens, expert_ids, gate_values, cotangent, w_gate, w_up, w_down):
    vmem = pl.BlockSpec(memory_space=pltpu.VMEM)
    hbm = pl.BlockSpec(memory_space=pl.ANY)
    dma = pltpu.SemaphoreType.DMA
    shapes = (
        jax.ShapeDtypeStruct((TOK, D), BF),
        jax.ShapeDtypeStruct((TOK, D), BF),
        jax.ShapeDtypeStruct((128, FF), F32),
        jax.ShapeDtypeStruct((128, FF), F32),
        jax.ShapeDtypeStruct((FF, 128), F32),
    )
    results = pl.pallas_call(
        kernel,
        out_shape=shapes,
        in_specs=[vmem] * 4 + [hbm] * 3,
        out_specs=(vmem,) * 5,
        scratch_shapes=[
            pltpu.VMEM((NZ, TOK, 2 * EXPERTS), BF),
            pltpu.VMEM((2, 2, NZ, TOK, HALF), BF),
            pltpu.VMEM((ROWS, GATHERED), BF),
            pltpu.VMEM((GATHERED, ROWS), BF),
            pltpu.VMEM((GATHERED, ROWS), BF),
            pltpu.VMEM((ROWS, 128), F32),
            pltpu.VMEM((4, ROWS, D), BF),
            pltpu.VMEM((4, ROWS, D), BF),
            pltpu.VMEM((ROWS, FF), F32),
            pltpu.VMEM((ROWS, FF), F32),
            pltpu.VMEM((ROWS, FF), BF),
            pltpu.VMEM((ROWS, 2 * FF), BF),
            pltpu.VMEM((2, GATHERED, D), F32),
            pltpu.VMEM((2, 2, 2, 5, TOK, HALF), BF),
            pltpu.VMEM((D, 2 * FF), F32),
            pltpu.VMEM((FF, D), F32),
            pltpu.VMEM((2, 2, 5, 128, FF), BF),
            pltpu.VMEM((2, 5, FF, 128), BF),
            pltpu.VMEM((FF, ROWS), BF),
            pltpu.VMEM((D, ROWS), BF),
            pltpu.VMEM((D, FF), BF),
            pltpu.VMEM((D, FF), BF),
            pltpu.VMEM((FF, D), BF),
            dma((NZ,)), dma((NZ,)),
            dma((2, 2, NZ)), dma((2, 2, NZ)),
            dma((8, PEERS)), dma((8, PEERS)),
            dma((2, 2, 2, 5)), dma((2, 2, 2, 5)),
            dma((3, 2, 5)), dma((3, 2, 5)),
            dma((3,)),
        ],
        compiler_params=pltpu.CompilerParams(
            collective_id=0, has_side_effects=True, vmem_limit_bytes=58 * 1024 * 1024
        ),
        cost_estimate=pl.CostEstimate(flops=7_000_000_000, bytes_accessed=8_000_000, transcendentals=400_000),
    )(expert_ids.T, gate_values.T, tokens, cotangent, w_gate[0], w_up[0], w_down[0])
    out, dtok, dg, du, dd = pl.pallas_call(
        place,
        out_shape=shapes,
        in_specs=[vmem] * 5,
        out_specs=(vmem,) * 5,
    )(*results)
    return out, dtok, dg[None], du[None], dd[None]


def solution(mesh):
    rows = P(("dp", "expert"), None)
    weights = P("expert", None, None)
    return jax.shard_map(
        on_device,
        mesh=mesh,
        in_specs=(rows,) * 4 + (weights,) * 3,
        out_specs=(rows, rows, P("expert", "dp", None), P("expert", "dp", None), P("expert", None, "dp")),
        check_vma=False,
    )
```
